32 devices in a mesh: input: 8 (over z, core), crate: 4 (over y, x).
Axes of the slice: x: 2, y: 2, z: 4, core: 2. Of those that a mesh axis runs over, the one named last changes fastest.
Arguments:
- volts: bfloat16 [4, 16, 530432], P('crate', 'input'), may hold values from -6 to 6
- gains: bfloat16 [4, 16, 256], P('crate', 'input'), may hold values from -5 to 5
Outputs:
- visibility: float32 [128, 2, 64, 64], P('input', None, 'crate')
The draws below stay inside these ranges and needn't reach their ends.
All inputs are finite; a program needn't handle non-finite values.
Results may differ from the reference program's by a relative error of at most 0.0026.
Values may be sent and summed in bfloat16 or wider, within the bound.
A program may use at most 64 MiB of HBM per device.

```python
import math
import jax
import jax.numpy as jnp
from jax import lax

FRAME = 2048
TAPS = 4
SUB = 128
SUB_START = 256
SPEC = 256
ROWS_CRATE = 16
CRATES = 4
INPUTS = 64
SAMPLES = 530432


def levels(own_key, extent, shards, low, high):
    factor_of, own = 1.0, jax.random.fold_in(own_key, 6)
    for dim, parts in shards:
        draws = jnp.exp(jax.random.uniform(jax.random.fold_in(own, dim), (parts,), jnp.float32, low / len(shards), high / len(shards)))
        factor_of = factor_of * jnp.repeat(draws, extent[dim] // parts).reshape([-1 if axis == dim else 1 for axis in range(len(extent))])
    return factor_of


def scatter_about(stream_key, dims, width, reach, split=(), held_as=jnp.bfloat16):
    entries = width * jax.random.normal(stream_key, dims, jnp.float32)
    if split:
        entries = entries * levels(stream_key, dims, split, -0.22, 0.18)
    return jnp.clip(entries, -reach, reach).astype(held_as)


def setup_inputs(seed: int = 0) -> dict:
    seeds = jax.random.split(jax.random.key(seed), 3)
    return {
        "volts": scatter_about(seeds[0], (CRATES, ROWS_CRATE, SAMPLES), 1.0, 6.0, ((0, 4), (1, 8))),
        "gains": scatter_about(seeds[1], (CRATES, ROWS_CRATE, 2 * SUB), 1.0, 5.0, ((0, 4), (1, 8))),
    }


def window_table():
    length = TAPS * FRAME
    index = jnp.arange(length, dtype=jnp.float32)
    centred = (index - length / 2.0 + 0.5) / FRAME
    taper = 0.5 - 0.5 * jnp.cos(2.0 * math.pi * (index + 0.5) / length)
    return (jnp.sinc(centred) * taper).reshape(TAPS, FRAME)

def make_table():
    sample_idx = jnp.arange(FRAME, dtype=jnp.int32)
    chan_idx = SUB_START + jnp.arange(SUB, dtype=jnp.int32)
    product = sample_idx[:, None] * chan_idx[None, :] % FRAME
    phase = product.astype(jnp.float32) * (2.0 * math.pi / FRAME)
    norm_factor = 1.0 / math.sqrt(FRAME)
    return (jnp.concatenate([jnp.cos(phase), -jnp.sin(phase)], axis=1) * norm_factor).astype(jnp.bfloat16)

def channelize(volt_rows, gain_rows, window, dft_table):
    count = volt_rows.shape[0]
    frames = volt_rows.reshape(count, SPEC + TAPS - 1, FRAME).astype(jnp.float32)
    summed = jnp.zeros((count, SPEC, FRAME), jnp.float32)
    for tap_index in range(TAPS):
        summed = summed + window[tap_index][None, None, :] * frames[:, tap_index:tap_index + SPEC, :]
    weighted = summed.astype(jnp.bfloat16)
    raw_spec = jnp.dot(weighted.reshape(count * SPEC, FRAME), dft_table, preferred_element_type=jnp.float32)
    raw_spec = raw_spec.reshape(count, SPEC, 2 * SUB)
    gain_f = gain_rows.astype(jnp.float32)[:, None, :]
    real_part, imag_part = (raw_spec[..., :SUB], raw_spec[..., SUB:])
    gain_re, gain_im = (gain_f[..., :SUB], gain_f[..., SUB:])
    out_re = real_part * gain_re - imag_part * gain_im
    out_im = real_part * gain_im + imag_part * gain_re
    return jnp.stack([out_re, out_im], axis=2).astype(jnp.bfloat16)

def reference(volts, gains):
    window = window_table()
    dft_table = make_table()

    def per_crate(pair):
        return channelize(pair[0], pair[1], window, dft_table)
    spectra = lax.map(per_crate, (volts, gains))
    spectra = spectra.reshape(INPUTS, SPEC, 2, SUB).transpose(3, 0, 2, 1)

    def per_channel(chan_data):
        columns = chan_data.reshape(INPUTS, 2 * SPEC)
        flipped = jnp.concatenate([chan_data[:, 1], -chan_data[:, 0]], axis=-1)
        real_vis = jnp.dot(columns, columns.T, preferred_element_type=jnp.float32)
        imag_vis = jnp.dot(flipped, columns.T, preferred_element_type=jnp.float32)
        return jnp.stack([real_vis, imag_vis], axis=0) * (1.0 / SPEC)
    return lax.map(per_channel, spectra)
```

```python
import functools
import math

import jax
import jax.numpy as jnp
import ml_dtypes
import numpy as np
from jax import lax
from jax.experimental import pallas as pl
from jax.experimental.pallas import tpu as pltpu
from jax.sharding import PartitionSpec as P

FRAME = 2048
TAPS = 4
SUB = 128
SUB_START = 256
SPEC = 256
LANES = 128
COLS = FRAME // LANES
FROWS = 2 * COLS
QUAD = 4
MESH = pl.DeviceIdType.MESH
NT = (((1,), (1,)), ((), ()))


def window_np():
    length = TAPS * FRAME
    index = np.arange(length, dtype=np.float64)
    centred = (index - length / 2.0 + 0.5) / FRAME
    taper = 0.5 - 0.5 * np.cos(2.0 * math.pi * (index + 0.5) / length)
    return (np.sinc(centred) * taper).reshape(TAPS, FRAME).astype(np.float32)


def table_np():
    sample_idx = np.arange(FRAME)
    chan_idx = SUB_START + np.arange(SUB)
    phase = (sample_idx[:, None] * chan_idx[None, :] % FRAME) * (2.0 * math.pi / FRAME)
    table = np.concatenate([np.cos(phase), -np.sin(phase)], axis=1) / math.sqrt(FRAME)
    return table.astype(np.float32).astype(ml_dtypes.bfloat16)


def channelize(volt_rows, gain_rows, window, dft_table):
    count = volt_rows.shape[0]
    frames = volt_rows.reshape(count, SPEC + TAPS - 1, FRAME).astype(jnp.float32)
    summed = jnp.zeros((count, SPEC, FRAME), jnp.float32)
    for tap_index in range(TAPS):
        summed = (
            summed + window[tap_index][None, None, :] * frames[:, tap_index : tap_index + SPEC, :]
        )
    weighted = summed.astype(jnp.bfloat16)
    raw_spec = jnp.dot(
        weighted.reshape(count * SPEC, FRAME), dft_table, preferred_element_type=jnp.float32
    )
    raw_spec = raw_spec.reshape(count, SPEC, 2 * SUB)
    gain_f = gain_rows.astype(jnp.float32)[:, None, :]
    real_part, imag_part = (raw_spec[..., :SUB], raw_spec[..., SUB:])
    gain_re, gain_im = (gain_f[..., :SUB], gain_f[..., SUB:])
    out_re = real_part * gain_re - imag_part * gain_im
    out_im = real_part * gain_im + imag_part * gain_re
    return jnp.stack([out_re, out_im], axis=2).astype(jnp.bfloat16)


def general_shards(volts, gains):
    spectra = channelize(volts[0], gains[0], jnp.asarray(window_np()), jnp.asarray(table_np()))
    outgoing = spectra.transpose(3, 0, 2, 1)
    groups = lax.axis_size("input")
    channels = outgoing.shape[0] // groups
    local = lax.all_to_all(outgoing, "input", split_axis=0, concat_axis=1, tiled=True)
    rows = local.shape[1]
    columns = local.reshape(channels, rows, 2 * SPEC)
    flipped = jnp.concatenate([local[:, :, 1], -local[:, :, 0]], axis=-1)
    row_operand = jnp.stack([columns, flipped], axis=1)
    gathered = lax.all_gather(columns, "crate", axis=1, tiled=True)
    visibility = jnp.einsum(
        "fqrk,fck->fqrc", row_operand, gathered, preferred_element_type=jnp.float32
    )
    return visibility * (1.0 / SPEC)


def kernel(
    groups, crates, volts_hbm, gains_ref, window_ref, table_hbm, pick_hbm, out_ref,
    raw, table, pick, fir, outgoing, arrived, wide, vis_out, load_sem, table_sem, pick_sem,
    send_sem, recv_sem, vsend_sem, vrecv_sem,
):
    n = groups * crates
    g, r = lax.axis_index("input"), lax.axis_index("crate")
    own = g * crates + r
    source = r * groups + g

    pieces = load_sem.shape[0]
    step = SPEC // pieces

    def load(k):
        start = 0 if k == 0 else (k * step + TAPS - 1) * FROWS
        stop = ((k + 1) * step + TAPS - 1) * FROWS
        rows = pl.ds(start, stop - start)
        return pltpu.make_async_copy(volts_hbm.at[rows], raw.at[rows], load_sem.at[k])

    loads = [load(k) for k in range(pieces)]
    loads[0].start()
    table_load = pltpu.make_async_copy(table_hbm, table, table_sem)
    pick_load = pltpu.make_async_copy(pick_hbm, pick, pick_sem)
    for item in loads[1:]:
        item.start()
    table_load.start()
    pick_load.start()

    barrier = pltpu.get_barrier_semaphore()

    @pl.loop(1, n)
    def _(k):
        other = lax.rem(own + k, n)
        pl.semaphore_signal(
            barrier, inc=1, device_id=(other // crates, lax.rem(other, crates)), device_id_type=MESH
        )

    taps = [window_ref[p] for p in range(TAPS)]

    def frame(t):
        return raw[pl.ds(pl.multiple_of(t * FROWS, FROWS), FROWS), :].astype(jnp.float32)

    for k in range(pieces):
        loads[k].wait()

        def body(s, held, k=k):
            held = list(held)
            for u in range(8):
                t = k * step + s * 8 + u
                held.append(frame(t + TAPS - 1))
                total = taps[0] * held[0]
                for p in range(1, TAPS):
                    total = total + taps[p] * held[p]
                fir[pl.ds(pl.multiple_of(t * FROWS, FROWS), FROWS), :] = total
                held = held[1:]
            return tuple(held)

        lax.fori_loop(0, step // 8, body, tuple(frame(k * step + p) for p in range(TAPS - 1)))

    table_load.wait()
    pick_load.wait()
    halves = []
    for i in range(2):
        total = jnp.zeros((2 * SUB, SPEC), jnp.float32)
        for c in range(0, COLS, 2):
            weighted = jnp.concatenate(
                [fir[pl.ds(2 * (c + e) + i, SPEC, stride=FROWS), :] for e in range(2)], axis=1
            ).astype(jnp.bfloat16)
            total = total + lax.dot_general(
                table[:, c * LANES : (c + 2) * LANES], weighted, NT,
                preferred_element_type=jnp.float32,
            )
        spread = jnp.broadcast_to(
            gains_ref[i : i + 1, :].astype(jnp.float32), (LANES, 2 * SUB)
        ).astype(jnp.bfloat16)
        gain = lax.dot_general(pick[...], spread, NT, preferred_element_type=jnp.float32)
        straight = jnp.concatenate([gain[: 2 * SUB]] * (SPEC // LANES), axis=1)
        crossed = jnp.concatenate([gain[2 * SUB :]] * (SPEC // LANES), axis=1)
        total = total.reshape(n, 2 * QUAD, SPEC)
        swapped = jnp.concatenate([total[:, QUAD:], total[:, :QUAD]], axis=1)
        halves.append(
            total * straight.reshape(n, 2 * QUAD, SPEC) + swapped * crossed.reshape(n, 2 * QUAD, SPEC)
        )
    outgoing[...] = jnp.concatenate(halves, axis=1).astype(jnp.bfloat16)

    pl.semaphore_wait(barrier, n - 1)

    @pl.loop(1, n)
    def _(k):
        other = lax.rem(own + k, n)
        pltpu.make_async_remote_copy(
            src_ref=outgoing.at[other],
            dst_ref=arrived.at[source],
            send_sem=send_sem,
            recv_sem=recv_sem,
            device_id=(other // crates, lax.rem(other, crates)),
            device_id_type=MESH,
        ).start()

    arrived[source] = outgoing[own]
    rest = pl.ds(0, n - 1)
    pltpu.make_async_copy(outgoing.at[rest], arrived.at[rest], recv_sem).wait()

    blocks = SPEC // LANES
    for e in range(blocks):
        part = arrived[:, :, e * LANES : (e + 1) * LANES].astype(jnp.float32)
        wide[e] = part.reshape(wide.shape[1:])
    inputs = 2 * n
    rows = inputs // crates
    for q in range(QUAD):
        real = [wide[e, pl.ds(q, inputs, stride=2 * QUAD), :] for e in range(blocks)]
        imag = [wide[e, pl.ds(QUAD + q, inputs, stride=2 * QUAD), :] for e in range(blocks)]
        left = jnp.concatenate(real + imag, axis=1).astype(jnp.bfloat16)
        turned = jnp.concatenate([-x for x in imag] + real, axis=1).astype(jnp.bfloat16)
        right = jnp.concatenate([left, turned], axis=0)
        vis = lax.dot_general(left, right, NT, preferred_element_type=jnp.float32) * (1.0 / SPEC)
        vis_out[:, q] = vis.reshape(crates, rows, 2 * inputs)

    for k in range(1, crates):
        other = lax.rem(r + k, crates)
        pltpu.make_async_remote_copy(
            src_ref=vis_out.at[other],
            dst_ref=out_ref.at[r],
            send_sem=vsend_sem,
            recv_sem=vrecv_sem,
            device_id=(g, other),
            device_id_type=MESH,
        ).start()
    out_ref[r] = vis_out[r]
    rest_v = pl.ds(0, crates - 1)
    pltpu.make_async_copy(vis_out.at[rest_v], out_ref.at[rest_v], vrecv_sem).wait()
    pltpu.make_async_copy(vis_out.at[rest_v], out_ref.at[rest_v], vsend_sem).wait()
    pltpu.make_async_copy(outgoing.at[rest], arrived.at[rest], send_sem).wait()


def quad_shards(groups, crates, volts, gains):
    n = groups * crates
    inputs = 2 * n
    rows = inputs // crates
    order = np.arange(2 * SUB).reshape(2, n, QUAD).transpose(1, 0, 2).reshape(-1)
    table = np.ascontiguousarray(table_np().T[order])
    chan = order % SUB
    imag = order >= SUB
    pick = np.zeros((2, 2 * SUB, 2 * SUB), np.float32)
    at = np.arange(2 * SUB)
    pick[0, at, chan] = 1.0
    pick[1, at, SUB + chan] = np.where(imag, 1.0, -1.0)
    pick = pick.reshape(4 * SUB, 2 * SUB).astype(ml_dtypes.bfloat16)
    window = np.repeat(window_np().reshape(TAPS, COLS, LANES), 2, axis=1)
    frames = volts.shape[-1] // LANES
    stacked = volts.reshape(2, frames, LANES).transpose(1, 0, 2).reshape(2 * frames, LANES)
    hbm = pl.BlockSpec(memory_space=pltpu.HBM)
    vmem = pl.BlockSpec(memory_space=pltpu.VMEM)
    pieces = 4
    vis = pl.pallas_call(
        functools.partial(kernel, groups, crates),
        out_shape=jax.ShapeDtypeStruct((crates, QUAD, rows, 2 * inputs), jnp.float32),
        in_specs=[hbm, vmem, vmem, hbm, hbm],
        out_specs=vmem,
        scratch_shapes=[
            pltpu.VMEM((2 * frames, LANES), jnp.bfloat16),
            pltpu.VMEM((2 * SUB, FRAME), jnp.bfloat16),
            pltpu.VMEM((4 * SUB, 2 * SUB), jnp.bfloat16),
            pltpu.VMEM((SPEC * FROWS, LANES), jnp.float32),
            pltpu.VMEM((n, 4 * QUAD, SPEC), jnp.bfloat16),
            pltpu.VMEM((n, 4 * QUAD, SPEC), jnp.bfloat16),
            pltpu.VMEM((SPEC // LANES, n * 4 * QUAD, LANES), jnp.float32),
            pltpu.VMEM((crates, QUAD, rows, 2 * inputs), jnp.float32),
            pltpu.SemaphoreType.DMA((pieces,)),
            pltpu.SemaphoreType.DMA,
            pltpu.SemaphoreType.DMA,
            pltpu.SemaphoreType.DMA,
            pltpu.SemaphoreType.DMA,
            pltpu.SemaphoreType.DMA,
            pltpu.SemaphoreType.DMA,
        ],
        compiler_params=pltpu.CompilerParams(
            collective_id=0, has_side_effects=True, vmem_limit_bytes=40 * 1024 * 1024
        ),
    )(stacked, gains[0], jnp.asarray(window), jnp.asarray(table), jnp.asarray(pick))
    vis = vis.reshape(crates * QUAD, rows, 2, inputs)
    return vis.transpose(0, 2, 1, 3)


def solution(mesh):
    groups, crates = mesh.shape["input"], mesh.shape["crate"]
    shards = general_shards
    if groups * crates * QUAD == SUB:
        shards = functools.partial(quad_shards, groups, crates)
    return jax.shard_map(
        shards,
        mesh=mesh,
        in_specs=(P("crate", "input", None), P("crate", "input", None)),
        out_specs=P("input", None, "crate", None),
        check_vma=False,
    )
```

```python
import functools
import math

import jax
import jax.numpy as jnp
import ml_dtypes
import numpy as np
from jax import lax
from jax.experimental import pallas as pl
from jax.experimental.pallas import tpu as pltpu
from jax.sharding import PartitionSpec as P

FRAME = 2048
TAPS = 4
SUB = 128
SUB_START = 256
SPEC = 256
LANES = 128
COLS = FRAME // LANES
FROWS = 2 * COLS
QUAD = 4
CHUNKS = SPEC // LANES
STRIDE = FROWS + 1
MESH = pl.DeviceIdType.MESH
NT = (((1,), (1,)), ((), ()))


def window_np():
    length = TAPS * FRAME
    index = np.arange(length, dtype=np.float64)
    centred = (index - length / 2.0 + 0.5) / FRAME
    taper = 0.5 - 0.5 * np.cos(2.0 * math.pi * (index + 0.5) / length)
    return (np.sinc(centred) * taper).reshape(TAPS, FRAME).astype(np.float32)


def table_np():
    sample_idx = np.arange(FRAME)
    chan_idx = SUB_START + np.arange(SUB)
    phase = (sample_idx[:, None] * chan_idx[None, :] % FRAME) * (2.0 * math.pi / FRAME)
    table = np.concatenate([np.cos(phase), -np.sin(phase)], axis=1) / math.sqrt(FRAME)
    return table.astype(np.float32).astype(ml_dtypes.bfloat16)


def channelize(volt_rows, gain_rows, window, dft_table):
    count = volt_rows.shape[0]
    frames = volt_rows.reshape(count, SPEC + TAPS - 1, FRAME).astype(jnp.float32)
    summed = jnp.zeros((count, SPEC, FRAME), jnp.float32)
    for tap_index in range(TAPS):
        summed = (
            summed + window[tap_index][None, None, :] * frames[:, tap_index : tap_index + SPEC, :]
        )
    weighted = summed.astype(jnp.bfloat16)
    raw_spec = jnp.dot(
        weighted.reshape(count * SPEC, FRAME), dft_table, preferred_element_type=jnp.float32
    )
    raw_spec = raw_spec.reshape(count, SPEC, 2 * SUB)
    gain_f = gain_rows.astype(jnp.float32)[:, None, :]
    real_part, imag_part = (raw_spec[..., :SUB], raw_spec[..., SUB:])
    gain_re, gain_im = (gain_f[..., :SUB], gain_f[..., SUB:])
    out_re = real_part * gain_re - imag_part * gain_im
    out_im = real_part * gain_im + imag_part * gain_re
    return jnp.stack([out_re, out_im], axis=2).astype(jnp.bfloat16)


def general_shards(volts, gains):
    spectra = channelize(volts[0], gains[0], jnp.asarray(window_np()), jnp.asarray(table_np()))
    outgoing = spectra.transpose(3, 0, 2, 1)
    groups = lax.axis_size("input")
    channels = outgoing.shape[0] // groups
    local = lax.all_to_all(outgoing, "input", split_axis=0, concat_axis=1, tiled=True)
    rows = local.shape[1]
    columns = local.reshape(channels, rows, 2 * SPEC)
    flipped = jnp.concatenate([local[:, :, 1], -local[:, :, 0]], axis=-1)
    row_operand = jnp.stack([columns, flipped], axis=1)
    gathered = lax.all_gather(columns, "crate", axis=1, tiled=True)
    visibility = jnp.einsum(
        "fqrk,fck->fqrc", row_operand, gathered, preferred_element_type=jnp.float32
    )
    return visibility * (1.0 / SPEC)


def kernel(
    groups, crates, volts_hbm, gains_hbm, window_hbm, table_hbm, pick_hbm, out_ref,
    raw, gains_ref, window_ref, table, pick, fir, outgoing, arrived, wide, vis_out, vis_in, load_sem, side_sem,
    send_sem, recv_sem, vsend_sem, vrecv_sem,
):
    n = groups * crates
    g, r = lax.axis_index("input"), lax.axis_index("crate")
    own = g * crates + r
    source = r * groups + g

    pieces = load_sem.shape[0]
    step = SPEC // pieces

    def load(k):
        start = 0 if k == 0 else (k * step + TAPS - 1) * FROWS
        stop = ((k + 1) * step + TAPS - 1) * FROWS
        rows = pl.ds(start, stop - start)
        return pltpu.make_async_copy(volts_hbm.at[rows], raw.at[rows], load_sem.at[k])

    loads = [load(k) for k in range(pieces)]
    sides = [
        pltpu.make_async_copy(src, dst, side_sem.at[k])
        for k, (src, dst) in enumerate(
            [(window_hbm, window_ref), (gains_hbm, gains_ref), (pick_hbm, pick), (table_hbm, table)]
        )
    ]
    head = pieces // CHUNKS
    for item in [*sides[:3], *loads[:head], sides[3], *loads[head:]]:
        item.start()

    barrier = pltpu.get_barrier_semaphore()

    @pl.loop(1, n)
    def _(k):
        other = lax.rem(own + k, n)
        pl.semaphore_signal(
            barrier, inc=1, device_id=(other // crates, lax.rem(other, crates)), device_id_type=MESH
        )

    sides[1].wait()
    sides[2].wait()
    gain = []
    for i in range(2):
        spread = jnp.broadcast_to(
            gains_ref[i : i + 1, :].astype(jnp.float32), (LANES, 2 * SUB)
        ).astype(jnp.bfloat16)
        spread = lax.dot_general(pick[...], spread, NT, preferred_element_type=jnp.float32)
        gain.append(spread.reshape(2, n, 2 * QUAD, LANES))

    sides[0].wait()
    taps = [window_ref[p] for p in range(TAPS)]

    def frame(t):
        return raw[pl.ds(pl.multiple_of(t * FROWS, FROWS), FROWS), :].astype(jnp.float32)

    def filtered(k):
        def body(s, held):
            held = list(held)
            base = pl.multiple_of((k * step + s * 8) * STRIDE, 8)
            for u in range(8):
                held.append(frame(k * step + s * 8 + u + TAPS - 1))
                total = taps[0] * held[0]
                for p in range(1, TAPS):
                    total = total + taps[p] * held[p]
                fir[pl.ds(base + u * STRIDE, FROWS), :] = total
                held = held[1:]
            return tuple(held)

        lax.fori_loop(0, step // 8, body, tuple(frame(k * step + p) for p in range(TAPS - 1)))

    span = SPEC // CHUNKS
    rest = pl.ds(0, n - 1)
    for h in range(CHUNKS):
        for k in range(h * head, (h + 1) * head):
            loads[k].wait()
            filtered(k)
        if h == 0:
            sides[3].wait()
        total = jnp.zeros((2 * SUB, 2 * span), jnp.float32)
        for c in range(0, COLS, 2):
            weighted = jnp.concatenate(
                [
                    jnp.concatenate(
                        [
                            fir[pl.ds(h * span * STRIDE + 2 * (c + e) + i, span, stride=STRIDE), :]
                            for e in range(2)
                        ],
                        axis=1,
                    )
                    for i in range(2)
                ],
                axis=0,
            ).astype(jnp.bfloat16)
            total = total + lax.dot_general(
                table[:, c * LANES : (c + 2) * LANES], weighted, NT,
                preferred_element_type=jnp.float32,
            )
        halves = []
        for i in range(2):
            part = total[:, i * span : (i + 1) * span].reshape(n, 2 * QUAD, span)
            swapped = jnp.concatenate([part[:, QUAD:], part[:, :QUAD]], axis=1)
            halves.append(part * gain[i][0] + swapped * gain[i][1])
        outgoing[h] = jnp.concatenate(halves, axis=1).astype(jnp.bfloat16)

        if h == 0:
            pl.semaphore_wait(barrier, n - 1)

        @pl.loop(1, n)
        def _(k, h=h):
            other = lax.rem(own + k, n)
            pltpu.make_async_remote_copy(
                src_ref=outgoing.at[h, other],
                dst_ref=arrived.at[h, source],
                send_sem=send_sem.at[h],
                recv_sem=recv_sem.at[h],
                device_id=(other // crates, lax.rem(other, crates)),
                device_id_type=MESH,
            ).start()

        arrived[h, source] = outgoing[h, own]

    for h in range(CHUNKS):
        pltpu.make_async_copy(outgoing.at[h, rest], arrived.at[h, rest], recv_sem.at[h]).wait()
        wide[h, : n * 4 * QUAD] = arrived[h].astype(jnp.float32).reshape(n * 4 * QUAD, LANES)

    inputs = 2 * n
    rows = inputs // crates
    for q in range(QUAD):
        real = [wide[h, pl.ds(q, inputs, stride=2 * QUAD), :] for h in range(CHUNKS)]
        imag = [wide[h, pl.ds(QUAD + q, inputs, stride=2 * QUAD), :] for h in range(CHUNKS)]
        left = jnp.concatenate(real + imag, axis=1).astype(jnp.bfloat16)
        turned = jnp.concatenate([-x for x in imag] + real, axis=1).astype(jnp.bfloat16)
        right = jnp.concatenate([left, turned], axis=0)
        vis = lax.dot_general(left, right, NT, preferred_element_type=jnp.float32) * (1.0 / SPEC)
        vis_out[:, q] = vis.reshape(crates, rows, 2 * inputs)
        for k in range(1, crates):
            other = lax.rem(r + k, crates)
            pltpu.make_async_remote_copy(
                src_ref=vis_out.at[other, q],
                dst_ref=vis_in.at[r, q],
                send_sem=vsend_sem,
                recv_sem=vrecv_sem,
                device_id=(g, other),
                device_id_type=MESH,
            ).start()

    vis_in[r] = vis_out[r]
    rest_v = pl.ds(0, crates - 1)
    pltpu.make_async_copy(vis_out.at[rest_v], vis_in.at[rest_v], vrecv_sem).wait()
    whole = vis_in[...].reshape(crates * QUAD, rows, 2 * inputs)
    out_ref[:, 0] = whole[:, :, :inputs]
    out_ref[:, 1] = whole[:, :, inputs:]
    pltpu.make_async_copy(vis_out.at[rest_v], vis_in.at[rest_v], vsend_sem).wait()
    for h in range(CHUNKS):
        pltpu.make_async_copy(outgoing.at[h, rest], arrived.at[h, rest], send_sem.at[h]).wait()


def quad_shards(groups, crates, volts, gains):
    n = groups * crates
    inputs = 2 * n
    rows = inputs // crates
    order = np.arange(2 * SUB).reshape(2, n, QUAD).transpose(1, 0, 2).reshape(-1)
    table = np.ascontiguousarray(table_np().T[order])
    chan = order % SUB
    imag = order >= SUB
    pick = np.zeros((2, 2 * SUB, 2 * SUB), np.float32)
    at = np.arange(2 * SUB)
    pick[0, at, chan] = 1.0
    pick[1, at, SUB + chan] = np.where(imag, 1.0, -1.0)
    pick = pick.reshape(4 * SUB, 2 * SUB).astype(ml_dtypes.bfloat16)
    window = np.repeat(window_np().reshape(TAPS, COLS, LANES), 2, axis=1)
    frames = volts.shape[-1] // LANES
    stacked = volts.reshape(2, frames, LANES).transpose(1, 0, 2).reshape(2 * frames, LANES)
    hbm = pl.BlockSpec(memory_space=pltpu.HBM)
    vmem = pl.BlockSpec(memory_space=pltpu.VMEM)
    pieces = 4
    return pl.pallas_call(
        functools.partial(kernel, groups, crates),
        out_shape=jax.ShapeDtypeStruct((crates * QUAD, 2, rows, inputs), jnp.float32),
        in_specs=[hbm] * 5,
        out_specs=vmem,
        scratch_shapes=[
            pltpu.VMEM((2 * frames, LANES), jnp.bfloat16),
            pltpu.VMEM((2, 2 * SUB), jnp.bfloat16),
            pltpu.VMEM((TAPS, FROWS, LANES), jnp.float32),
            pltpu.VMEM((2 * SUB, FRAME), jnp.bfloat16),
            pltpu.VMEM((4 * SUB, 2 * SUB), jnp.bfloat16),
            pltpu.VMEM(((SPEC + 2) * STRIDE, LANES), jnp.float32),
            pltpu.VMEM((CHUNKS, n, 4 * QUAD, LANES), jnp.bfloat16),
            pltpu.VMEM((CHUNKS, n, 4 * QUAD, LANES), jnp.bfloat16),
            pltpu.VMEM((CHUNKS, (n + 1) * 4 * QUAD, LANES), jnp.float32),
            pltpu.VMEM((crates, QUAD, rows, 2 * inputs), jnp.float32),
            pltpu.VMEM((crates, QUAD, rows, 2 * inputs), jnp.float32),
            pltpu.SemaphoreType.DMA((pieces,)),
            pltpu.SemaphoreType.DMA((4,)),
            pltpu.SemaphoreType.DMA((CHUNKS,)),
            pltpu.SemaphoreType.DMA((CHUNKS,)),
            pltpu.SemaphoreType.DMA,
            pltpu.SemaphoreType.DMA,
        ],
        compiler_params=pltpu.CompilerParams(
            collective_id=0, has_side_effects=True, vmem_limit_bytes=60 * 1024 * 1024
        ),
    )(stacked, gains[0], jnp.asarray(window), jnp.asarray(table), jnp.asarray(pick))


def solution(mesh):
    groups, crates = mesh.shape["input"], mesh.shape["crate"]
    shards = general_shards
    if groups * crates * QUAD == SUB:
        shards = functools.partial(quad_shards, groups, crates)
    return jax.shard_map(
        shards,
        mesh=mesh,
        in_specs=(P("crate", "input", None), P("crate", "input", None)),
        out_specs=P("input", None, "crate", None),
        check_vma=False,
    )
```

```python
import functools
import math

import jax
import jax.numpy as jnp
import ml_dtypes
import numpy as np
from jax import lax
from jax.experimental import pallas as pl
from jax.experimental.pallas import tpu as pltpu
from jax.sharding import PartitionSpec as P

FRAME = 2048
TAPS = 4
SUB = 128
SUB_START = 256
SPEC = 256
LANES = 128
COLS = FRAME // LANES
FROWS = 2 * COLS
QUAD = 4
CHUNKS = SPEC // LANES
STRIDE = FROWS + 1
MESH = pl.DeviceIdType.MESH
NT = (((1,), (1,)), ((), ()))


def window_np():
    length = TAPS * FRAME
    index = np.arange(length, dtype=np.float64)
    centred = (index - length / 2.0 + 0.5) / FRAME
    taper = 0.5 - 0.5 * np.cos(2.0 * math.pi * (index + 0.5) / length)
    return (np.sinc(centred) * taper).reshape(TAPS, FRAME).astype(np.float32)


def table_np():
    sample_idx = np.arange(FRAME)
    chan_idx = SUB_START + np.arange(SUB)
    phase = (sample_idx[:, None] * chan_idx[None, :] % FRAME) * (2.0 * math.pi / FRAME)
    table = np.concatenate([np.cos(phase), -np.sin(phase)], axis=1) / math.sqrt(FRAME)
    return table.astype(np.float32).astype(ml_dtypes.bfloat16)


def channelize(volt_rows, gain_rows, window, dft_table):
    count = volt_rows.shape[0]
    frames = volt_rows.reshape(count, SPEC + TAPS - 1, FRAME).astype(jnp.float32)
    summed = jnp.zeros((count, SPEC, FRAME), jnp.float32)
    for tap_index in range(TAPS):
        summed = (
            summed + window[tap_index][None, None, :] * frames[:, tap_index : tap_index + SPEC, :]
        )
    weighted = summed.astype(jnp.bfloat16)
    raw_spec = jnp.dot(
        weighted.reshape(count * SPEC, FRAME), dft_table, preferred_element_type=jnp.float32
    )
    raw_spec = raw_spec.reshape(count, SPEC, 2 * SUB)
    gain_f = gain_rows.astype(jnp.float32)[:, None, :]
    real_part, imag_part = (raw_spec[..., :SUB], raw_spec[..., SUB:])
    gain_re, gain_im = (gain_f[..., :SUB], gain_f[..., SUB:])
    out_re = real_part * gain_re - imag_part * gain_im
    out_im = real_part * gain_im + imag_part * gain_re
    return jnp.stack([out_re, out_im], axis=2).astype(jnp.bfloat16)


def general_shards(volts, gains):
    spectra = channelize(volts[0], gains[0], jnp.asarray(window_np()), jnp.asarray(table_np()))
    outgoing = spectra.transpose(3, 0, 2, 1)
    groups = lax.axis_size("input")
    channels = outgoing.shape[0] // groups
    local = lax.all_to_all(outgoing, "input", split_axis=0, concat_axis=1, tiled=True)
    rows = local.shape[1]
    columns = local.reshape(channels, rows, 2 * SPEC)
    flipped = jnp.concatenate([local[:, :, 1], -local[:, :, 0]], axis=-1)
    row_operand = jnp.stack([columns, flipped], axis=1)
    gathered = lax.all_gather(columns, "crate", axis=1, tiled=True)
    visibility = jnp.einsum(
        "fqrk,fck->fqrc", row_operand, gathered, preferred_element_type=jnp.float32
    )
    return visibility * (1.0 / SPEC)


def kernel(
    groups, crates, volts_hbm, gains_hbm, window_hbm, table_hbm, pick_hbm, out_ref,
    raw, gains_ref, window_ref, table, pick, fir, outgoing, arrived, wide, vis_out, vis_in, load_sem, side_sem,
    send_sem, recv_sem, vsend_sem, vrecv_sem,
):
    n = groups * crates
    g, r = lax.axis_index("input"), lax.axis_index("crate")
    own = g * crates + r
    source = r * groups + g

    pieces = load_sem.shape[0]
    step = SPEC // pieces

    def load(k):
        start = 0 if k == 0 else (k * step + TAPS - 1) * FROWS
        stop = ((k + 1) * step + TAPS - 1) * FROWS
        rows = pl.ds(start, stop - start)
        return pltpu.make_async_copy(volts_hbm.at[rows], raw.at[rows], load_sem.at[k])

    loads = [load(k) for k in range(pieces)]
    sides = [
        pltpu.make_async_copy(src, dst, side_sem.at[k])
        for k, (src, dst) in enumerate(
            [(window_hbm, window_ref), (gains_hbm, gains_ref), (pick_hbm, pick), (table_hbm, table)]
        )
    ]
    head = pieces // CHUNKS
    for item in [*sides[:3], *loads[:head], sides[3], *loads[head:]]:
        item.start()

    barrier = pltpu.get_barrier_semaphore()

    @pl.loop(1, n)
    def _(k):
        other = lax.rem(own + k, n)
        pl.semaphore_signal(
            barrier, inc=1, device_id=(other // crates, lax.rem(other, crates)), device_id_type=MESH
        )

    sides[1].wait()
    sides[2].wait()
    gain = []
    for i in range(2):
        spread = jnp.broadcast_to(
            gains_ref[i : i + 1, :].astype(jnp.float32), (LANES, 2 * SUB)
        ).astype(jnp.bfloat16)
        spread = lax.dot_general(pick[...], spread, NT, preferred_element_type=jnp.float32)
        gain.append(spread.reshape(2, n, 2 * QUAD, LANES))

    sides[0].wait()
    taps = [window_ref[p] for p in range(TAPS)]

    def frame(t):
        return raw[pl.ds(pl.multiple_of(t * FROWS, FROWS), FROWS), :].astype(jnp.float32)

    def filtered(k):
        def body(s, held):
            held = list(held)
            base = pl.multiple_of((k * step + s * 8) * STRIDE, 8)
            for u in range(8):
                held.append(frame(k * step + s * 8 + u + TAPS - 1))
                total = taps[0] * held[0]
                for p in range(1, TAPS):
                    total = total + taps[p] * held[p]
                fir[pl.ds(base + u * STRIDE, FROWS), :] = total
                held = held[1:]
            return tuple(held)

        lax.fori_loop(0, step // 8, body, tuple(frame(k * step + p) for p in range(TAPS - 1)))

    span = SPEC // CHUNKS
    rest = pl.ds(0, n - 1)
    for h in range(CHUNKS):
        for k in range(h * head, (h + 1) * head):
            loads[k].wait()
            filtered(k)
        if h == 0:
            sides[3].wait()
        total = jnp.zeros((2 * SUB, 2 * span), jnp.float32)
        for c in range(0, COLS, 2):
            weighted = jnp.concatenate(
                [
                    jnp.concatenate(
                        [
                            fir[pl.ds(h * span * STRIDE + 2 * (c + e) + i, span, stride=STRIDE), :]
                            for e in range(2)
                        ],
                        axis=1,
                    )
                    for i in range(2)
                ],
                axis=0,
            ).astype(jnp.bfloat16)
            total = total + lax.dot_general(
                table[:, c * LANES : (c + 2) * LANES], weighted, NT,
                preferred_element_type=jnp.float32,
            )
        halves = []
        for i in range(2):
            part = total[:, i * span : (i + 1) * span].reshape(n, 2 * QUAD, span)
            swapped = jnp.concatenate([part[:, QUAD:], part[:, :QUAD]], axis=1)
            halves.append(part * gain[i][0] + swapped * gain[i][1])
        outgoing[h] = jnp.concatenate(halves, axis=1).astype(jnp.bfloat16)

        if h == 0:
            pl.semaphore_wait(barrier, n - 1)

        @pl.loop(1, n)
        def _(k, h=h):
            other = lax.rem(own + k, n)
            pltpu.make_async_remote_copy(
                src_ref=outgoing.at[h, other],
                dst_ref=arrived.at[h, source],
                send_sem=send_sem.at[h],
                recv_sem=recv_sem.at[h],
                device_id=(other // crates, lax.rem(other, crates)),
                device_id_type=MESH,
            ).start()

        arrived[h, source] = outgoing[h, own]

    for h in range(CHUNKS):
        pltpu.make_async_copy(outgoing.at[h, rest], arrived.at[h, rest], recv_sem.at[h]).wait()
        wide[h, : n * 4 * QUAD] = arrived[h].astype(jnp.float32).reshape(n * 4 * QUAD, LANES)

    inputs = 2 * n
    rows = inputs // crates
    for q in range(QUAD):
        real = [wide[h, pl.ds(q, inputs, stride=2 * QUAD), :] for h in range(CHUNKS)]
        imag = [wide[h, pl.ds(QUAD + q, inputs, stride=2 * QUAD), :] for h in range(CHUNKS)]
        left = jnp.concatenate(real + imag, axis=1).astype(jnp.bfloat16)
        turned = jnp.concatenate([-x for x in imag] + real, axis=1).astype(jnp.bfloat16)
        right = jnp.concatenate([left, turned], axis=0)
        vis = lax.dot_general(left, right, NT, preferred_element_type=jnp.float32) * (1.0 / SPEC)
        vis_out[:, q] = vis.reshape(crates, rows, 2 * inputs)
        for k in range(1, crates):
            other = lax.rem(r + k, crates)
            pltpu.make_async_remote_copy(
                src_ref=vis_out.at[other, q],
                dst_ref=vis_in.at[r, q],
                send_sem=vsend_sem,
                recv_sem=vrecv_sem,
                device_id=(g, other),
                device_id_type=MESH,
            ).start()

    vis_in[r] = vis_out[r]
    rest_v = pl.ds(0, crates - 1)
    pltpu.make_async_copy(vis_out.at[rest_v], vis_in.at[rest_v], vrecv_sem).wait()
    whole = vis_in[...].reshape(crates * QUAD, rows, 2 * inputs)
    out_ref[:, 0] = whole[:, :, :inputs]
    out_ref[:, 1] = whole[:, :, inputs:]
    pltpu.make_async_copy(vis_out.at[rest_v], vis_in.at[rest_v], vsend_sem).wait()
    for h in range(CHUNKS):
        pltpu.make_async_copy(outgoing.at[h, rest], arrived.at[h, rest], send_sem.at[h]).wait()


def quad_shards(groups, crates, volts, gains):
    n = groups * crates
    inputs = 2 * n
    rows = inputs // crates
    order = np.arange(2 * SUB).reshape(2, n, QUAD).transpose(1, 0, 2).reshape(-1)
    table = np.ascontiguousarray(table_np().T[order])
    chan = order % SUB
    imag = order >= SUB
    pick = np.zeros((2, 2 * SUB, 2 * SUB), np.float32)
    at = np.arange(2 * SUB)
    pick[0, at, chan] = 1.0
    pick[1, at, SUB + chan] = np.where(imag, 1.0, -1.0)
    pick = pick.reshape(4 * SUB, 2 * SUB).astype(ml_dtypes.bfloat16)
    window = np.repeat(window_np().reshape(TAPS, COLS, LANES), 2, axis=1)
    frames = volts.shape[-1] // LANES
    stacked = volts.reshape(2, frames, LANES).transpose(1, 0, 2).reshape(2 * frames, LANES)
    hbm = pl.BlockSpec(memory_space=pltpu.HBM)
    vmem = pl.BlockSpec(memory_space=pltpu.VMEM)
    pieces = 4
    return pl.pallas_call(
        functools.partial(kernel, groups, crates),
        out_shape=pltpu.VMEM((crates * QUAD, 2, rows, inputs), jnp.float32),
        in_specs=[hbm] * 5,
        out_specs=vmem,
        scratch_shapes=[
            pltpu.VMEM((2 * frames, LANES), jnp.bfloat16),
            pltpu.VMEM((2, 2 * SUB), jnp.bfloat16),
            pltpu.VMEM((TAPS, FROWS, LANES), jnp.float32),
            pltpu.VMEM((2 * SUB, FRAME), jnp.bfloat16),
            pltpu.VMEM((4 * SUB, 2 * SUB), jnp.bfloat16),
            pltpu.VMEM(((SPEC + 2) * STRIDE, LANES), jnp.float32),
            pltpu.VMEM((CHUNKS, n, 4 * QUAD, LANES), jnp.bfloat16),
            pltpu.VMEM((CHUNKS, n, 4 * QUAD, LANES), jnp.bfloat16),
            pltpu.VMEM((CHUNKS, (n + 1) * 4 * QUAD, LANES), jnp.float32),
            pltpu.VMEM((crates, QUAD, rows, 2 * inputs), jnp.float32),
            pltpu.VMEM((crates, QUAD, rows, 2 * inputs), jnp.float32),
            pltpu.SemaphoreType.DMA((pieces,)),
            pltpu.SemaphoreType.DMA((4,)),
            pltpu.SemaphoreType.DMA((CHUNKS,)),
            pltpu.SemaphoreType.DMA((CHUNKS,)),
            pltpu.SemaphoreType.DMA,
            pltpu.SemaphoreType.DMA,
        ],
        compiler_params=pltpu.CompilerParams(
            collective_id=0, has_side_effects=True, vmem_limit_bytes=57000000
        ),
    )(stacked, gains[0], jnp.asarray(window), jnp.asarray(table), jnp.asarray(pick))


def solution(mesh):
    groups, crates = mesh.shape["input"], mesh.shape["crate"]
    shards = general_shards
    if groups * crates * QUAD == SUB:
        shards = functools.partial(quad_shards, groups, crates)
    return jax.shard_map(
        shards,
        mesh=mesh,
        in_specs=(P("crate", "input", None), P("crate", "input", None)),
        out_specs=P("input", None, "crate", None),
        check_vma=False,
    )
```

```python
import functools
import math

import jax
import jax.numpy as jnp
import ml_dtypes
import numpy as np
from jax import lax
from jax.experimental import pallas as pl
from jax.experimental.pallas import tpu as pltpu
from jax.sharding import PartitionSpec as P

FRAME = 2048
TAPS = 4
SUB = 128
SUB_START = 256
SPEC = 256
LANES = 128
COLS = FRAME // LANES
FROWS = 2 * COLS
QUAD = 4
CHUNKS = SPEC // LANES
STRIDE = FROWS + 1
MESH = pl.DeviceIdType.MESH
NT = (((1,), (1,)), ((), ()))


def window_np():
    length = TAPS * FRAME
    index = np.arange(length, dtype=np.float64)
    centred = (index - length / 2.0 + 0.5) / FRAME
    taper = 0.5 - 0.5 * np.cos(2.0 * math.pi * (index + 0.5) / length)
    return (np.sinc(centred) * taper).reshape(TAPS, FRAME).astype(np.float32)


def table_np():
    sample_idx = np.arange(FRAME)
    chan_idx = SUB_START + np.arange(SUB)
    phase = (sample_idx[:, None] * chan_idx[None, :] % FRAME) * (2.0 * math.pi / FRAME)
    table = np.concatenate([np.cos(phase), -np.sin(phase)], axis=1) / math.sqrt(FRAME)
    return table.astype(np.float32).astype(ml_dtypes.bfloat16)


def channelize(volt_rows, gain_rows, window, dft_table):
    count = volt_rows.shape[0]
    frames = volt_rows.reshape(count, SPEC + TAPS - 1, FRAME).astype(jnp.float32)
    summed = jnp.zeros((count, SPEC, FRAME), jnp.float32)
    for tap_index in range(TAPS):
        summed = (
            summed + window[tap_index][None, None, :] * frames[:, tap_index : tap_index + SPEC, :]
        )
    weighted = summed.astype(jnp.bfloat16)
    raw_spec = jnp.dot(
        weighted.reshape(count * SPEC, FRAME), dft_table, preferred_element_type=jnp.float32
    )
    raw_spec = raw_spec.reshape(count, SPEC, 2 * SUB)
    gain_f = gain_rows.astype(jnp.float32)[:, None, :]
    real_part, imag_part = (raw_spec[..., :SUB], raw_spec[..., SUB:])
    gain_re, gain_im = (gain_f[..., :SUB], gain_f[..., SUB:])
    out_re = real_part * gain_re - imag_part * gain_im
    out_im = real_part * gain_im + imag_part * gain_re
    return jnp.stack([out_re, out_im], axis=2).astype(jnp.bfloat16)


def general_shards(volts, gains):
    spectra = channelize(volts[0], gains[0], jnp.asarray(window_np()), jnp.asarray(table_np()))
    outgoing = spectra.transpose(3, 0, 2, 1)
    groups = lax.axis_size("input")
    channels = outgoing.shape[0] // groups
    local = lax.all_to_all(outgoing, "input", split_axis=0, concat_axis=1, tiled=True)
    rows = local.shape[1]
    columns = local.reshape(channels, rows, 2 * SPEC)
    flipped = jnp.concatenate([local[:, :, 1], -local[:, :, 0]], axis=-1)
    row_operand = jnp.stack([columns, flipped], axis=1)
    gathered = lax.all_gather(columns, "crate", axis=1, tiled=True)
    visibility = jnp.einsum(
        "fqrk,fck->fqrc", row_operand, gathered, preferred_element_type=jnp.float32
    )
    return visibility * (1.0 / SPEC)


def kernel(
    groups, crates, volts_hbm, gains_hbm, window_hbm, table_hbm, pick_hbm, out_ref,
    raw, gains_ref, window_ref, table, pick, fir, outgoing, arrived, wide, vis_out, vis_in, load_sem, side_sem,
    send_sem, recv_sem, vsend_sem, vrecv_sem,
):
    n = groups * crates
    g, r = lax.axis_index("input"), lax.axis_index("crate")
    own = g * crates + r
    source = r * groups + g

    pieces = load_sem.shape[0]
    step = SPEC // pieces

    def load(k):
        start = 0 if k == 0 else (k * step + TAPS - 1) * FROWS
        stop = ((k + 1) * step + TAPS - 1) * FROWS
        rows = pl.ds(start, stop - start)
        return pltpu.make_async_copy(volts_hbm.at[rows], raw.at[rows], load_sem.at[k])

    loads = [load(k) for k in range(pieces)]
    sides = [
        pltpu.make_async_copy(src, dst, side_sem.at[k])
        for k, (src, dst) in enumerate(
            [(window_hbm, window_ref), (gains_hbm, gains_ref), (pick_hbm, pick), (table_hbm, table)]
        )
    ]
    head = pieces // CHUNKS
    for item in [*sides[:3], *loads[:head]]:
        item.start()

    barrier = pltpu.get_barrier_semaphore()

    near_g = [lax.rem(g + k, groups) for k in range(groups)]
    near_r = [lax.rem(r + k, crates) for k in range(crates)]
    for k in reversed(range(1, n)):
        pl.semaphore_signal(
            barrier, inc=1, device_id=(near_g[k // crates], near_r[k % crates]), device_id_type=MESH
        )

    for item in [sides[3], *loads[head:]]:
        item.start()

    sides[1].wait()
    sides[2].wait()
    gain = []
    for i in range(2):
        spread = jnp.broadcast_to(
            gains_ref[i : i + 1, :].astype(jnp.float32), (LANES, 2 * SUB)
        ).astype(jnp.bfloat16)
        spread = lax.dot_general(pick[...], spread, NT, preferred_element_type=jnp.float32)
        gain.append(spread.reshape(2, n, 2 * QUAD, LANES))

    sides[0].wait()
    taps = [window_ref[p] for p in range(TAPS)]

    def frame(t):
        return raw[pl.ds(pl.multiple_of(t * FROWS, FROWS), FROWS), :].astype(jnp.float32)

    def filtered(k):
        def body(s, held):
            held = list(held)
            base = pl.multiple_of((k * step + s * 8) * STRIDE, 8)
            for u in range(8):
                held.append(frame(k * step + s * 8 + u + TAPS - 1))
                total = taps[0] * held[0]
                for p in range(1, TAPS):
                    total = total + taps[p] * held[p]
                fir[pl.ds(base + u * STRIDE, FROWS), :] = total
                held = held[1:]
            return tuple(held)

        lax.fori_loop(0, step // 8, body, tuple(frame(k * step + p) for p in range(TAPS - 1)))

    span = SPEC // CHUNKS
    rest = pl.ds(0, n - 1)
    for h in range(CHUNKS):
        for k in range(h * head, (h + 1) * head):
            loads[k].wait()
            filtered(k)
        if h == 0:
            sides[3].wait()
        total = jnp.zeros((2 * SUB, 2 * span), jnp.float32)
        for c in range(0, COLS, 2):
            weighted = jnp.concatenate(
                [
                    jnp.concatenate(
                        [
                            fir[pl.ds(h * span * STRIDE + 2 * (c + e) + i, span, stride=STRIDE), :]
                            for e in range(2)
                        ],
                        axis=1,
                    )
                    for i in range(2)
                ],
                axis=0,
            ).astype(jnp.bfloat16)
            total = total + lax.dot_general(
                table[:, c * LANES : (c + 2) * LANES], weighted, NT,
                preferred_element_type=jnp.float32,
            )
        halves = []
        for i in range(2):
            part = total[:, i * span : (i + 1) * span].reshape(n, 2 * QUAD, span)
            swapped = jnp.concatenate([part[:, QUAD:], part[:, :QUAD]], axis=1)
            halves.append(part * gain[i][0] + swapped * gain[i][1])
        outgoing[h] = jnp.concatenate(halves, axis=1).astype(jnp.bfloat16)

        if h == 0:
            pl.semaphore_wait(barrier, n - 1)

        @pl.loop(1, n)
        def _(k, h=h):
            other = lax.rem(own + k, n)
            pltpu.make_async_remote_copy(
                src_ref=outgoing.at[h, other],
                dst_ref=arrived.at[h, source],
                send_sem=send_sem.at[h],
                recv_sem=recv_sem.at[h],
                device_id=(other // crates, lax.rem(other, crates)),
                device_id_type=MESH,
            ).start()

        arrived[h, source] = outgoing[h, own]

    inputs = 2 * n
    rows = inputs // crates
    sums = [0.0] * QUAD
    for h in range(CHUNKS):
        pltpu.make_async_copy(outgoing.at[h, rest], arrived.at[h, rest], recv_sem.at[h]).wait()
        wide[h, : n * 4 * QUAD] = arrived[h].astype(jnp.float32).reshape(n * 4 * QUAD, LANES)
        for q in range(QUAD):
            real = wide[h, pl.ds(q, inputs, stride=2 * QUAD), :]
            imag = wide[h, pl.ds(QUAD + q, inputs, stride=2 * QUAD), :]
            left = jnp.concatenate([real, imag], axis=1).astype(jnp.bfloat16)
            turned = jnp.concatenate([-imag, real], axis=1).astype(jnp.bfloat16)
            right = jnp.concatenate([left, turned], axis=0)
            sums[q] = sums[q] + lax.dot_general(
                left, right, NT, preferred_element_type=jnp.float32
            )
    for q in range(QUAD):
        vis = sums[q] * (1.0 / SPEC)
        vis_out[:, q] = vis.reshape(crates, rows, 2 * inputs)

    for k in range(1, crates):
        other = lax.rem(r + k, crates)
        pltpu.make_async_remote_copy(
            src_ref=vis_out.at[other],
            dst_ref=vis_in.at[r],
            send_sem=vsend_sem,
            recv_sem=vrecv_sem,
            device_id=(g, other),
            device_id_type=MESH,
        ).start()

    vis_in[r] = vis_out[r]
    rest_v = pl.ds(0, crates - 1)
    pltpu.make_async_copy(vis_out.at[rest_v], vis_in.at[rest_v], vrecv_sem).wait()
    whole = vis_in[...].reshape(crates * QUAD, rows, 2 * inputs)
    out_ref[:, 0] = whole[:, :, :inputs]
    out_ref[:, 1] = whole[:, :, inputs:]
    pltpu.make_async_copy(vis_out.at[rest_v], vis_in.at[rest_v], vsend_sem).wait()
    for h in range(CHUNKS):
        pltpu.make_async_copy(outgoing.at[h, rest], arrived.at[h, rest], send_sem.at[h]).wait()


def quad_shards(groups, crates, volts, gains):
    n = groups * crates
    inputs = 2 * n
    rows = inputs // crates
    order = np.arange(2 * SUB).reshape(2, n, QUAD).transpose(1, 0, 2).reshape(-1)
    table = np.ascontiguousarray(table_np().T[order])
    chan = order % SUB
    imag = order >= SUB
    pick = np.zeros((2, 2 * SUB, 2 * SUB), np.float32)
    at = np.arange(2 * SUB)
    pick[0, at, chan] = 1.0
    pick[1, at, SUB + chan] = np.where(imag, 1.0, -1.0)
    pick = pick.reshape(4 * SUB, 2 * SUB).astype(ml_dtypes.bfloat16)
    window = np.repeat(window_np().reshape(TAPS, COLS, LANES), 2, axis=1)
    frames = volts.shape[-1] // LANES
    stacked = volts.reshape(2, frames, LANES).transpose(1, 0, 2).reshape(2 * frames, LANES)
    hbm = pl.BlockSpec(memory_space=pltpu.HBM)
    vmem = pl.BlockSpec(memory_space=pltpu.VMEM)
    pieces = 2
    return pl.pallas_call(
        functools.partial(kernel, groups, crates),
        out_shape=pltpu.VMEM((crates * QUAD, 2, rows, inputs), jnp.float32),
        in_specs=[hbm] * 5,
        out_specs=vmem,
        scratch_shapes=[
            pltpu.VMEM((2 * frames, LANES), jnp.bfloat16),
            pltpu.VMEM((2, 2 * SUB), jnp.bfloat16),
            pltpu.VMEM((TAPS, FROWS, LANES), jnp.float32),
            pltpu.VMEM((2 * SUB, FRAME), jnp.bfloat16),
            pltpu.VMEM((4 * SUB, 2 * SUB), jnp.bfloat16),
            pltpu.VMEM(((SPEC + 2) * STRIDE, LANES), jnp.float32),
            pltpu.VMEM((CHUNKS, n, 4 * QUAD, LANES), jnp.bfloat16),
            pltpu.VMEM((CHUNKS, n, 4 * QUAD, LANES), jnp.bfloat16),
            pltpu.VMEM((CHUNKS, (n + 1) * 4 * QUAD, LANES), jnp.float32),
            pltpu.VMEM((crates, QUAD, rows, 2 * inputs), jnp.float32),
            pltpu.VMEM((crates, QUAD, rows, 2 * inputs), jnp.float32),
            pltpu.SemaphoreType.DMA((pieces,)),
            pltpu.SemaphoreType.DMA((4,)),
            pltpu.SemaphoreType.DMA((CHUNKS,)),
            pltpu.SemaphoreType.DMA((CHUNKS,)),
            pltpu.SemaphoreType.DMA,
            pltpu.SemaphoreType.DMA,
        ],
        compiler_params=pltpu.CompilerParams(
            collective_id=0, has_side_effects=True, vmem_limit_bytes=57000000
        ),
    )(stacked, gains[0], jnp.asarray(window), jnp.asarray(table), jnp.asarray(pick))


def solution(mesh):
    groups, crates = mesh.shape["input"], mesh.shape["crate"]
    shards = general_shards
    if groups * crates * QUAD == SUB:
        shards = functools.partial(quad_shards, groups, crates)
    return jax.shard_map(
        shards,
        mesh=mesh,
        in_specs=(P("crate", "input", None), P("crate", "input", None)),
        out_specs=P("input", None, "crate", None),
        check_vma=False,
    )
```
